32 devices in a mesh: row: 4 (over y, core), col: 8 (over z, x).
Axes of the slice: x: 2, y: 2, z: 4, core: 2. Of those that a mesh axis runs over, the one named last changes fastest.
Arguments:
- tokens: bfloat16 [128, 128, 192], P('row', 'col'), may hold values from -6 to 6
- tissue: int32 [128, 128], P('row', 'col'), may hold values 0 or 1
- ln_gain: float32 [192], replicated, may hold values from 0.5 to 1.5
- in_weight: bfloat16 [192, 768], replicated, may hold values from -0.4375 to 0.4375
- conv_weight: bfloat16 [3, 3, 384], replicated, may hold values from -2 to 2
- conv_bias: float32 [384], replicated, may hold values from -3 to 3
- proj_weight: bfloat16 [4, 384, 44], replicated, may hold values from -0.3125 to 0.3125
- dt_weight: bfloat16 [4, 12, 384], replicated, may hold values from -1.75 to 1.75
- dt_bias: float32 [4, 384], replicated, may hold values from -4 to -1
- a_rate: float32 [4, 384, 16], replicated, may hold values from 0.001 to 1
- skip_d: float32 [4, 384], replicated, may hold values from 0.5 to 1.5
- out_gain: float32 [384], replicated, may hold values from 0.5 to 1.5
- out_weight: bfloat16 [384, 192], replicated, may hold values from -0.3125 to 0.3125
Outputs:
- result: bfloat16 [128, 128, 192], P('row', 'col')
The draws below stay inside these ranges and needn't reach their ends.
Inputs may be any that keep to these rules, and one draw needn't show every extreme that they name: 1 marks a tissue token, 0 a background token.
All inputs are finite; a program needn't handle non-finite values. No bound on the sum of `tissue` on one device may be relied on, other than what follows from the above.
Results may differ from the reference program's by a relative error of at most 0.0055.
Values may be sent and summed in bfloat16 or wider, within the bound.
A program may use at most 256 MiB of HBM per device.

```python
import math
import jax
import jax.numpy as jnp
from jax import lax

D = 192
E = 384
NSTATE = 16
RANK = 12
HEIGHT = 128
WIDTH = 128


def plant(result, stream_key, least, high):
    index_at = [jax.random.randint(jax.random.fold_in(stream_key, axis), (), 0, length) for axis, length in enumerate(result.shape)]
    main_axis = result.shape.index(max(result.shape))
    next_to = index_at[:main_axis] + [(index_at[main_axis] + 1) % result.shape[main_axis]] + index_at[main_axis + 1:]
    return result.at[tuple(index_at)].set(least).at[tuple(next_to)].set(high)


def steps_of(key, dims, cuts, smallest, top_value):
    factor_of, own = 1.0, jax.random.fold_in(key, 6)
    for axis_at, blocks in cuts:
        heights = jnp.exp(jax.random.uniform(jax.random.fold_in(own, axis_at), (blocks,), jnp.float32, smallest / len(cuts), top_value / len(cuts)))
        factor_of = factor_of * jnp.repeat(heights, dims[axis_at] // blocks).reshape([-1 if axis == axis_at else 1 for axis in range(len(dims))])
    return factor_of


def scatter_about(rng, dims, deviation, limit, pieces=(), kind=jnp.bfloat16):
    drawn = deviation * jax.random.normal(rng, dims, jnp.float32)
    if pieces:
        drawn = drawn * steps_of(rng, dims, pieces, -0.22, 0.18)
    return jnp.clip(drawn, -limit, limit).astype(kind)


def setup_inputs(seed: int = 0) -> dict:
    seeds = jax.random.split(jax.random.key(seed), 14)
    tokens = scatter_about(seeds[0], (HEIGHT, WIDTH, D), 1.0, 6.0, ((0, 4), (1, 8)))
    tissue = plant((jax.random.randint(seeds[1], (HEIGHT, WIDTH), 0, 4) < 3).astype(jnp.int32), jax.random.fold_in(seeds[1], 1), 0, 1)
    ln_gain = jnp.clip(1.0 + 0.1 * jax.random.normal(seeds[2], (D,), jnp.float32), 0.5, 1.5)
    in_weight = scatter_about(seeds[3], (D, 2 * E), D ** -0.5, 0.4375)
    conv_weight = scatter_about(seeds[4], (3, 3, E), 9 ** -0.5, 2.0)
    conv_bias = scatter_about(seeds[5], (E,), 0.5, 3.0, (), jnp.float32)
    proj_weight = scatter_about(seeds[6], (4, E, RANK + 2 * NSTATE), E ** -0.5, 0.3125)
    dt_weight = scatter_about(seeds[7], (4, RANK, E), RANK ** -0.5, 1.75)
    dt_bias = jnp.clip(jax.random.uniform(seeds[8], (4, E), jnp.float32, -4.0, -1.0), -4.0, -1.0)
    a_rate = jnp.clip(jnp.exp(jax.random.uniform(seeds[9], (4, E, NSTATE), jnp.float32, math.log(0.001), math.log(1.0))), 0.001, 1.0)
    skip_d = jnp.clip(jax.random.uniform(seeds[10], (4, E), jnp.float32, 0.5, 1.5), 0.5, 1.5)
    out_gain = jnp.clip(1.0 + 0.1 * jax.random.normal(seeds[11], (E,), jnp.float32), 0.5, 1.5)
    out_weight = scatter_about(seeds[12], (E, D), E ** -0.5, 0.3125)
    return {"tokens": tokens, "tissue": tissue, "ln_gain": ln_gain, "in_weight": in_weight, "conv_weight": conv_weight, "conv_bias": conv_bias, "proj_weight": proj_weight, "dt_weight": dt_weight, "dt_bias": dt_bias, "a_rate": a_rate, "skip_d": skip_d, "out_gain": out_gain, "out_weight": out_weight}


def layer_norm(values, gain):
    center = values - lax.optimization_barrier(jnp.mean(values, axis=-1, keepdims=True))
    spread = lax.optimization_barrier(jnp.mean(center * center, axis=-1, keepdims=True))
    return center * lax.rsqrt(spread + 1e-05) * gain

def conv_silu(padded, conv_weight, conv_bias, height, width):
    summed = jnp.broadcast_to(conv_bias.astype(jnp.float32), (height, width, conv_bias.shape[0]))
    for offset_row in range(3):
        for offset_col in range(3):
            window = padded[offset_row:offset_row + height, offset_col:offset_col + width]
            summed = summed + window.astype(jnp.float32) * conv_weight[offset_row, offset_col].astype(jnp.float32)
    return jax.nn.silu(summed).astype(jnp.bfloat16)

def direction_inputs(conv_out, tissue_wide, proj_one, dtw_one, dtb_one):
    rank = dtw_one.shape[0]
    nstate = (proj_one.shape[1] - rank) // 2
    rows, cols, inner = conv_out.shape
    flat = conv_out.reshape(rows * cols, inner)
    projections = jnp.dot(flat, proj_one, preferred_element_type=jnp.float32)
    rate_low = projections[:, :rank].astype(jnp.bfloat16)
    delta = jax.nn.softplus(jnp.dot(rate_low, dtw_one, preferred_element_type=jnp.float32) + dtb_one)
    delta = delta.reshape(rows, cols, inner) * tissue_wide[:, :, None]
    entry = projections[:, rank:rank + nstate].reshape(rows, cols, nstate)
    readout = projections[:, rank + nstate:].reshape(rows, cols, nstate)
    return (delta, entry, readout)

def to_seq(array, axis, flip):
    moved = jnp.moveaxis(array, axis, 0)
    if flip:
        moved = moved[::-1]
    return moved

def from_seq(array, axis, flip):
    if flip:
        array = array[::-1]
    return jnp.moveaxis(array, 0, axis)

def scan_steps(conv_seq, delta_seq, entry_seq, readout_seq, rates, skip_gain, initial):

    def advance(state, inputs):
        conv_now, delta_now, entry_now, readout_now = inputs
        conv_wide = conv_now.astype(jnp.float32)
        state = jnp.exp(-delta_now[:, :, None] * rates) * state + (delta_now * conv_wide)[:, :, None] * entry_now[:, None, :]
        output = lax.optimization_barrier(jnp.sum(state * readout_now[:, None, :], axis=2)) + skip_gain * conv_wide
        return (state, output)
    _, outputs = lax.scan(advance, initial, (conv_seq, delta_seq, entry_seq, readout_seq))
    return outputs

def run_local(conv_out, inputs, rates, skip_gain, axis, flip):
    delta, entry, readout = inputs
    conv_seq = to_seq(conv_out, axis, flip)
    initial = jnp.zeros((conv_seq.shape[1], rates.shape[0], rates.shape[1]), jnp.float32)
    outputs = scan_steps(conv_seq, to_seq(delta, axis, flip), to_seq(entry, axis, flip), to_seq(readout, axis, flip), rates, skip_gain, initial)
    return from_seq(outputs, axis, flip)

def reference(tokens, tissue, ln_gain, in_weight, conv_weight, conv_bias, proj_weight, dt_weight, dt_bias, a_rate, skip_d, out_gain, out_weight):
    height, width_cols, width = tokens.shape
    inner = in_weight.shape[1] // 2
    normed = layer_norm(tokens.astype(jnp.float32), ln_gain).astype(jnp.bfloat16)
    projected = jnp.dot(normed.reshape(height * width_cols, width), in_weight, preferred_element_type=jnp.float32)
    projected = projected.astype(jnp.bfloat16).reshape(height, width_cols, 2 * inner)
    inner_part = projected[:, :, :inner]
    gate_part = projected[:, :, inner:]
    padded = jnp.pad(inner_part, ((1, 1), (1, 1), (0, 0)))
    conv_out = conv_silu(padded, conv_weight, conv_bias, height, width_cols)
    tissue_wide = tissue.astype(jnp.float32)
    mixed_sum = jnp.zeros((height, width_cols, inner), jnp.float32)
    for direction in range(4):
        axis = 1 if direction % 2 == 0 else 0
        flip = direction >= 2
        inputs = direction_inputs(conv_out, tissue_wide, proj_weight[direction], dt_weight[direction], dt_bias[direction])
        mixed_sum = mixed_sum + run_local(conv_out, inputs, a_rate[direction], skip_d[direction], axis, flip)
    mixed = (layer_norm(mixed_sum, out_gain) * jax.nn.silu(gate_part.astype(jnp.float32))).astype(jnp.bfloat16)
    branch = jnp.dot(mixed.reshape(height * width_cols, inner), out_weight, preferred_element_type=jnp.float32)
    branch = branch.reshape(height, width_cols, width)
    return (tokens.astype(jnp.float32) + tissue_wide[:, :, None] * branch).astype(jnp.bfloat16)
```

```python
import functools
import math

import jax
import jax.numpy as jnp
from jax import lax
from jax.experimental import pallas as pl
from jax.experimental.pallas import tpu as pltpu
from jax.sharding import PartitionSpec as P

LANES = 128
GROUP = 8
STAGGER = 3
SPAN = 4
MESH = pl.DeviceIdType.MESH


def scan_kernel(
    rows, cols, x_ref, gate_ref, tok_ref, tis_ref, proj_ref, dtw_ref, dtb_ref, rate_ref, skip_ref,
    og_ref, ow_ref, out_ref, xs, dl, pj, ys, st, sbuf, rbuf, ssem, rsem
):
    nrow, ncol = lax.axis_size("row"), lax.axis_size("col")
    me_row, me_col = lax.axis_index("row"), lax.axis_index("col")
    count, inner = x_ref.shape
    tiles = inner // LANES
    rank = dtw_ref.shape[1]
    nstate = rate_ref.shape[1]

    barrier = pltpu.get_barrier_semaphore()
    near = (
        (me_col > 0, (me_row, me_col - 1)),
        (me_col < ncol - 1, (me_row, me_col + 1)),
        (me_row > 0, (me_row - 1, me_col)),
        (me_row < nrow - 1, (me_row + 1, me_col)),
    )
    expected = 0
    for there, device in near:
        expected = expected + there.astype(jnp.int32)

        @pl.when(there)
        def _():
            pl.semaphore_signal(barrier, inc=1, device_id=device, device_id_type=MESH)

    pl.semaphore_wait(barrier, expected)

    step = min(count, 128)

    def prepare(c, _):
        at = pl.ds(pl.multiple_of(c * step, step), step)
        block = x_ref[at, :]
        wide = block.astype(jnp.float32)
        mask = tis_ref[at, :]
        skip = jnp.sum(skip_ref[...], axis=0, keepdims=True)
        base = wide * skip
        for e in range(tiles):
            xs[e, at, :] = wide[:, e * LANES : (e + 1) * LANES]
            ys[e, at, :] = base[:, e * LANES : (e + 1) * LANES]
        for k in range(4):
            p = jnp.dot(block, proj_ref[k], preferred_element_type=jnp.float32)
            pj[k, at, : p.shape[1]] = p
            low = p[:, :rank].astype(jnp.bfloat16)
            z = jnp.dot(low, dtw_ref[k], preferred_element_type=jnp.float32) + dtb_ref[k : k + 1, :]
            delta = (jnp.maximum(z, 0.0) + jnp.log1p(jnp.exp(-jnp.abs(z)))) * mask
            for e in range(tiles):
                dl[k * tiles + e, at, :] = delta[:, e * LANES : (e + 1) * LANES]
        return 0

    lax.fori_loop(0, count // step, prepare, 0)

    row_units, col_units = rows // GROUP * tiles, cols // GROUP * tiles
    plans = (
        (0, me_col, (me_row, me_col + 1), ncol, row_units, 0),
        (2, ncol - 1 - me_col, (me_row, me_col - 1), ncol, row_units, row_units),
        (1, me_row, (me_row + 1, me_col), nrow, col_units, 2 * row_units),
        (3, nrow - 1 - me_row, (me_row - 1, me_col), nrow, col_units, 2 * row_units + col_units),
    )

    def copy_of(u, device):
        return pltpu.make_async_remote_copy(
            src_ref=sbuf.at[u],
            dst_ref=rbuf.at[u],
            send_sem=ssem.at[u],
            recv_sem=rsem.at[u],
            device_id=device,
            device_id_type=MESH,
        )

    def unit(k, ahead, device, size, first, q):
        g = q // tiles
        e = q % tiles
        u = first + q
        length = cols if k % 2 == 0 else rows

        @pl.when(ahead > 0)
        def _():
            copy_of(u, device).wait_recv()
            st[...] = rbuf[u].astype(jnp.float32)

        @pl.when(ahead == 0)
        def _():
            st[...] = jnp.zeros_like(st)

        rates = [
            jnp.broadcast_to(
                rate_ref[k, n : n + 1, pl.ds(pl.multiple_of(e * LANES, LANES), LANES)],
                (GROUP, LANES),
            )
            for n in range(nstate)
        ]
        lane = k * tiles + e

        def advance(block, state):
            state = list(state)
            for sub in range(SPAN):
                t = block * SPAN + sub
                if k >= 2:
                    t = length - 1 - t
                if k % 2 == 0:
                    at = pl.ds(g * (GROUP * cols) + t, GROUP, stride=cols)
                else:
                    at = pl.ds(pl.multiple_of(t * cols + g * GROUP, GROUP), GROUP)
                d = dl[lane, at, :]
                dx = d * xs[e, at, :]
                p = pj[k, at, :]
                parts = [None] * 4
                for n in range(nstate):
                    b = jnp.broadcast_to(p[:, rank + n : rank + n + 1], (GROUP, LANES))
                    r = jnp.broadcast_to(
                        p[:, rank + nstate + n : rank + nstate + n + 1], (GROUP, LANES)
                    )
                    state[n] = jnp.exp2(d * rates[n]) * state[n] + dx * b
                    term = state[n] * r
                    parts[n % 4] = term if parts[n % 4] is None else parts[n % 4] + term
                ys[e, at, :] += (parts[0] + parts[1]) + (parts[2] + parts[3])
            return tuple(state)

        state = tuple(st[n * GROUP : (n + 1) * GROUP, :] for n in range(nstate))
        state = lax.fori_loop(0, length // SPAN, advance, state)

        @pl.when(ahead < size - 1)
        def _():
            sbuf[u] = jnp.concatenate(state, axis=0).astype(jnp.bfloat16)
            copy_of(u, device).start()

    slots = max(STAGGER * (ncol - 1) + row_units, STAGGER * (nrow - 1) + col_units)

    def slot(s, _):
        for k, ahead, device, size, units, first in plans:
            q = s - STAGGER * ahead

            @pl.when((q >= 0) & (q < units))
            def _():
                unit(k, ahead, device, size, first, q)

        return 0

    lax.fori_loop(0, slots, slot, 0)

    def finish(c, _):
        at = pl.ds(pl.multiple_of(c * step, step), step)
        parts = [ys[e, at, :] for e in range(tiles)]
        mean = sum(jnp.sum(a, axis=1, keepdims=True) for a in parts) / inner
        parts = [a - mean for a in parts]
        spread = sum(jnp.sum(a * a, axis=1, keepdims=True) for a in parts) / inner
        scale = lax.rsqrt(spread + 1e-05)
        gate = gate_ref[at, :].astype(jnp.float32)
        gate = gate * jax.nn.sigmoid(gate) * og_ref[...]
        mixed = (jnp.concatenate(parts, axis=1) * scale * gate).astype(jnp.bfloat16)
        branch = jnp.dot(mixed, ow_ref[...], preferred_element_type=jnp.float32)
        out_ref[at, :] = (tok_ref[at, :].astype(jnp.float32) + tis_ref[at, :] * branch).astype(
            jnp.bfloat16
        )
        return 0

    lax.fori_loop(0, count // step, finish, 0)

    for k, ahead, device, size, units, first in plans:

        @pl.when(ahead < size - 1)
        def _():
            def drain(q, _):
                copy_of(first + q, device).wait_send()
                return 0

            lax.fori_loop(0, units, drain, 0)


def mix(x, gate, tokens, tissue, proj, dtw, dtb, rate, skip, og, ow, rows, cols):
    count, inner = x.shape
    tiles = inner // LANES
    nstate = rate.shape[1]
    units = 2 * tiles * (rows // GROUP + cols // GROUP)
    held = (units, nstate * GROUP, LANES)
    return pl.pallas_call(
        functools.partial(scan_kernel, rows, cols),
        out_shape=jax.ShapeDtypeStruct((count, ow.shape[1]), jnp.bfloat16),
        in_specs=[pl.BlockSpec(memory_space=pltpu.VMEM)] * 11,
        out_specs=pl.BlockSpec(memory_space=pltpu.VMEM),
        scratch_shapes=[
            pltpu.VMEM((tiles, count, LANES), jnp.float32),
            pltpu.VMEM((4 * tiles, count, LANES), jnp.float32),
            pltpu.VMEM((4, count, LANES), jnp.float32),
            pltpu.VMEM((tiles, count, LANES), jnp.float32),
            pltpu.VMEM((nstate * GROUP, LANES), jnp.float32),
            pltpu.VMEM(held, jnp.bfloat16),
            pltpu.VMEM(held, jnp.bfloat16),
            pltpu.SemaphoreType.DMA((units,)),
            pltpu.SemaphoreType.DMA((units,)),
        ],
        compiler_params=pltpu.CompilerParams(
            collective_id=0, has_side_effects=True, vmem_limit_bytes=40 * 1024 * 1024
        ),
    )(x, gate, tokens, tissue, proj, dtw, dtb, rate, skip, og, ow)


def padded_2(block, sides, width):
    for axis, dim in sides:
        count = lax.axis_size(axis)
        forward = [(i, i + 1) for i in range(count - 1)]
        backward = [(target, source) for source, target in forward]
        low = lax.ppermute(
            lax.slice_in_dim(block, block.shape[dim] - width, None, axis=dim), axis, forward
        )
        high = lax.ppermute(lax.slice_in_dim(block, 0, width, axis=dim), axis, backward)
        block = jnp.concatenate([low, block, high], axis=dim)
    return block


def layer_norm(values, gain):
    center = values - jnp.mean(values, axis=-1, keepdims=True)
    spread = jnp.mean(center * center, axis=-1, keepdims=True)
    return center * lax.rsqrt(spread + 1e-05) * gain


def conv_silu(padded, conv_weight, conv_bias, height, width):
    summed = jnp.broadcast_to(conv_bias, (height, width, conv_bias.shape[0]))
    for offset_row in range(3):
        for offset_col in range(3):
            window = padded[offset_row : offset_row + height, offset_col : offset_col + width]
            summed = summed + window.astype(jnp.float32) * conv_weight[
                offset_row, offset_col
            ].astype(jnp.float32)
    return jax.nn.silu(summed).astype(jnp.bfloat16)


def local(
    tokens,
    tissue,
    ln_gain,
    in_weight,
    conv_weight,
    conv_bias,
    proj_weight,
    dt_weight,
    dt_bias,
    a_rate,
    skip_d,
    out_gain,
    out_weight,
):
    rows_here, cols_here, width = tokens.shape
    inner = in_weight.shape[1] // 2
    normed = layer_norm(tokens.astype(jnp.float32), ln_gain).astype(jnp.bfloat16)
    projected = jnp.dot(
        normed.reshape(rows_here * cols_here, width), in_weight, preferred_element_type=jnp.float32
    )
    projected = projected.astype(jnp.bfloat16).reshape(rows_here, cols_here, 2 * inner)
    inner_part = projected[:, :, :inner]
    gate_part = projected[:, :, inner:]
    padded = padded_2(inner_part, (("row", 0), ("col", 1)), 1)
    conv_out = conv_silu(padded, conv_weight, conv_bias, rows_here, cols_here)
    count = rows_here * cols_here
    out = mix(
        conv_out.reshape(count, inner),
        gate_part.reshape(count, inner),
        tokens.reshape(count, width),
        tissue.astype(jnp.float32).reshape(count, 1),
        proj_weight,
        dt_weight,
        dt_bias,
        a_rate.transpose(0, 2, 1) * (-1.0 / math.log(2.0)),
        skip_d,
        out_gain.reshape(1, inner),
        out_weight,
        rows_here,
        cols_here,
    )
    return out.reshape(rows_here, cols_here, width)


def solution(mesh):
    return jax.shard_map(
        local,
        mesh=mesh,
        in_specs=(
            P("row", "col", None),
            P("row", "col"),
            P(),
            P(),
            P(),
            P(),
            P(),
            P(),
            P(),
            P(),
            P(),
            P(),
            P(),
        ),
        out_specs=P("row", "col", None),
        check_vma=False,
    )
```

```python
import functools
import math

import jax
import jax.numpy as jnp
from jax import lax
from jax.experimental import pallas as pl
from jax.experimental.pallas import tpu as pltpu
from jax.sharding import PartitionSpec as P

LANES = 128
GROUP = 8
STAGGER = 3
SPAN = 4
MESH = pl.DeviceIdType.MESH


def spread_out(rows, cols, rank, nstate, pj, pk, ex):
    count = rows * cols

    def reorder(i, _):
        t, g = i // (rows // GROUP), i % (rows // GROUP)
        source = pl.ds(g * (GROUP * cols) + t, GROUP, stride=cols)
        target = pl.ds(pl.multiple_of(t * rows + g * GROUP, GROUP), GROUP)
        for k in (0, 2):
            ex[k, 0, target, :] = pj[k, source, :]
        return 0

    lax.fori_loop(0, count // GROUP, reorder, 0)
    for k in range(4):
        for c in range(count // 128):
            at = pl.ds(c * 128, 128)
            value = pj[k, at, :] if k % 2 else ex[k, 0, at, :]
            high = value.astype(jnp.bfloat16)
            low = (value - high.astype(jnp.float32)).astype(jnp.bfloat16)
            pk[k, at, :LANES] = high
            pk[k, at, LANES:] = low

    source = lax.broadcasted_iota(jnp.int32, (2 * LANES, 2 * LANES), 0) % LANES
    target = lax.broadcasted_iota(jnp.int32, (2 * LANES, 2 * LANES), 1) // LANES

    def pair(m, _):
        pick = (source == target + (rank + 2 * m)).astype(jnp.bfloat16)
        for k in range(4):
            for c in range(count // 256):
                at = pl.ds(c * 256, 256)
                value = jnp.dot(pk[k, at, :], pick, preferred_element_type=jnp.float32)
                ex[k, 2 * m, at, :] = value[:, :LANES]
                ex[k, 2 * m + 1, at, :] = value[:, LANES:]
        return 0

    lax.fori_loop(0, nstate, pair, 0)


def scan_kernel(
    rows, cols, x_ref, gate_ref, tok_ref, tis_ref, proj_ref, dtw_ref, dtb_ref, rate_ref, skip_ref,
    og_ref, ow_ref, out_ref, xs, dl, pj, ys, st, sbuf, rbuf, ssem, rsem, *wide_refs
):
    nrow, ncol = lax.axis_size("row"), lax.axis_size("col")
    me_row, me_col = lax.axis_index("row"), lax.axis_index("col")
    count, inner = x_ref.shape
    tiles = inner // LANES
    rank = dtw_ref.shape[1]
    nstate = rate_ref.shape[1]

    barrier = pltpu.get_barrier_semaphore()
    near = (
        (me_col > 0, (me_row, me_col - 1)),
        (me_col < ncol - 1, (me_row, me_col + 1)),
        (me_row > 0, (me_row - 1, me_col)),
        (me_row < nrow - 1, (me_row + 1, me_col)),
    )
    expected = 0
    for there, device in near:
        expected = expected + there.astype(jnp.int32)

        @pl.when(there)
        def _():
            pl.semaphore_signal(barrier, inc=1, device_id=device, device_id_type=MESH)

    pl.semaphore_wait(barrier, expected)

    step = min(count, 128)

    def prepare(c, _):
        at = pl.ds(pl.multiple_of(c * step, step), step)
        block = x_ref[at, :]
        wide = block.astype(jnp.float32)
        mask = tis_ref[at, :]
        skip = jnp.sum(skip_ref[...], axis=0, keepdims=True)
        base = wide * skip
        for e in range(tiles):
            xs[e, at, :] = wide[:, e * LANES : (e + 1) * LANES]
            ys[e, at, :] = base[:, e * LANES : (e + 1) * LANES]
        for k in range(4):
            p = jnp.dot(block, proj_ref[k], preferred_element_type=jnp.float32)
            pj[k, at, :] = jnp.concatenate(
                [p, jnp.zeros((step, LANES - p.shape[1]), jnp.float32)], axis=1
            )
            low = p[:, :rank].astype(jnp.bfloat16)
            z = jnp.dot(low, dtw_ref[k], preferred_element_type=jnp.float32) + dtb_ref[k : k + 1, :]
            delta = (jnp.maximum(z, 0.0) + jnp.log1p(jnp.exp(-jnp.abs(z)))) * mask
            for e in range(tiles):
                dl[k * tiles + e, at, :] = delta[:, e * LANES : (e + 1) * LANES]
        return 0

    lax.fori_loop(0, count // step, prepare, 0)

    if wide_refs:
        spread_out(rows, cols, rank, nstate, pj, *wide_refs)
    row_units, col_units = rows // GROUP * tiles, cols // GROUP * tiles
    plans = (
        (0, me_col, (me_row, me_col + 1), ncol, row_units, 0),
        (2, ncol - 1 - me_col, (me_row, me_col - 1), ncol, row_units, row_units),
        (1, me_row, (me_row + 1, me_col), nrow, col_units, 2 * row_units),
        (3, nrow - 1 - me_row, (me_row - 1, me_col), nrow, col_units, 2 * row_units + col_units),
    )

    def copy_of(u, device):
        return pltpu.make_async_remote_copy(
            src_ref=sbuf.at[u],
            dst_ref=rbuf.at[u],
            send_sem=ssem.at[u],
            recv_sem=rsem.at[u],
            device_id=device,
            device_id_type=MESH,
        )

    def unit(k, ahead, device, size, first, q):
        g = q // tiles
        e = q % tiles
        u = first + q
        length = cols if k % 2 == 0 else rows

        @pl.when(ahead > 0)
        def _():
            copy_of(u, device).wait_recv()
            st[...] = rbuf[u].astype(jnp.float32)

        @pl.when(ahead == 0)
        def _():
            st[...] = jnp.zeros_like(st)

        rates = [
            jnp.broadcast_to(
                rate_ref[k, n : n + 1, pl.ds(pl.multiple_of(e * LANES, LANES), LANES)],
                (GROUP, LANES),
            )
            for n in range(nstate)
        ]
        lane = k * tiles + e

        def advance(block, state):
            state = list(state)
            for sub in range(SPAN):
                t = block * SPAN + sub
                if k >= 2:
                    t = length - 1 - t
                if k % 2 == 0:
                    at = pl.ds(g * (GROUP * cols) + t, GROUP, stride=cols)
                else:
                    at = pl.ds(pl.multiple_of(t * cols + g * GROUP, GROUP), GROUP)
                d = dl[lane, at, :]
                dx = d * xs[e, at, :]
                if wide_refs:
                    ex = wide_refs[1]
                    where = at
                    if k % 2 == 0:
                        where = pl.ds(pl.multiple_of(t * rows + g * GROUP, GROUP), GROUP)
                    wide = [ex[k, m, where, :] for m in range(2 * nstate)]
                else:
                    p = pj[k, at, :]
                    wide = [
                        jnp.broadcast_to(p[:, rank + m : rank + m + 1], (GROUP, LANES))
                        for m in range(2 * nstate)
                    ]
                parts = [None] * 4
                for n in range(nstate):
                    state[n] = jnp.exp2(d * rates[n]) * state[n] + dx * wide[n]
                    term = state[n] * wide[nstate + n]
                    parts[n % 4] = term if parts[n % 4] is None else parts[n % 4] + term
                ys[e, at, :] += (parts[0] + parts[1]) + (parts[2] + parts[3])
            return tuple(state)

        state = tuple(st[n * GROUP : (n + 1) * GROUP, :] for n in range(nstate))
        state = lax.fori_loop(0, length // SPAN, advance, state)

        @pl.when(ahead < size - 1)
        def _():
            sbuf[u] = jnp.concatenate(state, axis=0).astype(jnp.bfloat16)
            copy_of(u, device).start()

    slots = max(STAGGER * (ncol - 1) + row_units, STAGGER * (nrow - 1) + col_units)

    def slot(s, _):
        for k, ahead, device, size, units, first in plans:
            q = s - STAGGER * ahead

            @pl.when((q >= 0) & (q < units))
            def _():
                unit(k, ahead, device, size, first, q)

        return 0

    lax.fori_loop(0, slots, slot, 0)

    def finish(c, _):
        at = pl.ds(pl.multiple_of(c * step, step), step)
        parts = [ys[e, at, :] for e in range(tiles)]
        mean = sum(jnp.sum(a, axis=1, keepdims=True) for a in parts) / inner
        parts = [a - mean for a in parts]
        spread = sum(jnp.sum(a * a, axis=1, keepdims=True) for a in parts) / inner
        scale = lax.rsqrt(spread + 1e-05)
        gate = gate_ref[at, :].astype(jnp.float32)
        gate = gate * jax.nn.sigmoid(gate) * og_ref[...]
        mixed = (jnp.concatenate(parts, axis=1) * scale * gate).astype(jnp.bfloat16)
        branch = jnp.dot(mixed, ow_ref[...], preferred_element_type=jnp.float32)
        out_ref[at, :] = (tok_ref[at, :].astype(jnp.float32) + tis_ref[at, :] * branch).astype(
            jnp.bfloat16
        )
        return 0

    lax.fori_loop(0, count // step, finish, 0)

    for k, ahead, device, size, units, first in plans:

        @pl.when(ahead < size - 1)
        def _():
            def drain(q, _):
                copy_of(first + q, device).wait_send()
                return 0

            lax.fori_loop(0, units, drain, 0)


def mix(x, gate, tokens, tissue, proj, dtw, dtb, rate, skip, og, ow, rows, cols):
    count, inner = x.shape
    tiles = inner // LANES
    nstate = rate.shape[1]
    units = 2 * tiles * (rows // GROUP + cols // GROUP)
    wide_shapes = []
    if count <= 512 and count % 256 == 0:
        wide_shapes = [
            pltpu.VMEM((4, count, 2 * LANES), jnp.bfloat16),
            pltpu.VMEM((4, 2 * nstate, count, LANES), jnp.float32),
        ]
    held = (units, nstate * GROUP, LANES)
    return pl.pallas_call(
        functools.partial(scan_kernel, rows, cols),
        out_shape=jax.ShapeDtypeStruct((count, ow.shape[1]), jnp.bfloat16),
        in_specs=[pl.BlockSpec(memory_space=pltpu.VMEM)] * 11,
        out_specs=pl.BlockSpec(memory_space=pltpu.VMEM),
        scratch_shapes=[
            pltpu.VMEM((tiles, count, LANES), jnp.float32),
            pltpu.VMEM((4 * tiles, count, LANES), jnp.float32),
            pltpu.VMEM((4, count, LANES), jnp.float32),
            pltpu.VMEM((tiles, count, LANES), jnp.float32),
            pltpu.VMEM((nstate * GROUP, LANES), jnp.float32),
            pltpu.VMEM(held, jnp.bfloat16),
            pltpu.VMEM(held, jnp.bfloat16),
            pltpu.SemaphoreType.DMA((units,)),
            pltpu.SemaphoreType.DMA((units,)),
            *wide_shapes,
        ],
        compiler_params=pltpu.CompilerParams(
            collective_id=0, has_side_effects=True, vmem_limit_bytes=56 * 1024 * 1024
        ),
    )(x, gate, tokens, tissue, proj, dtw, dtb, rate, skip, og, ow)


def padded_2(block, sides, width):
    for axis, dim in sides:
        count = lax.axis_size(axis)
        forward = [(i, i + 1) for i in range(count - 1)]
        backward = [(target, source) for source, target in forward]
        low = lax.ppermute(
            lax.slice_in_dim(block, block.shape[dim] - width, None, axis=dim), axis, forward
        )
        high = lax.ppermute(lax.slice_in_dim(block, 0, width, axis=dim), axis, backward)
        block = jnp.concatenate([low, block, high], axis=dim)
    return block


def layer_norm(values, gain):
    center = values - jnp.mean(values, axis=-1, keepdims=True)
    spread = jnp.mean(center * center, axis=-1, keepdims=True)
    return center * lax.rsqrt(spread + 1e-05) * gain


def conv_silu(padded, conv_weight, conv_bias, height, width):
    summed = jnp.broadcast_to(conv_bias, (height, width, conv_bias.shape[0]))
    for offset_row in range(3):
        for offset_col in range(3):
            window = padded[offset_row : offset_row + height, offset_col : offset_col + width]
            summed = summed + window.astype(jnp.float32) * conv_weight[
                offset_row, offset_col
            ].astype(jnp.float32)
    return jax.nn.silu(summed).astype(jnp.bfloat16)


def local(
    tokens,
    tissue,
    ln_gain,
    in_weight,
    conv_weight,
    conv_bias,
    proj_weight,
    dt_weight,
    dt_bias,
    a_rate,
    skip_d,
    out_gain,
    out_weight,
):
    rows_here, cols_here, width = tokens.shape
    inner = in_weight.shape[1] // 2
    normed = layer_norm(tokens.astype(jnp.float32), ln_gain).astype(jnp.bfloat16)
    projected = jnp.dot(
        normed.reshape(rows_here * cols_here, width), in_weight, preferred_element_type=jnp.float32
    )
    projected = projected.astype(jnp.bfloat16).reshape(rows_here, cols_here, 2 * inner)
    inner_part = projected[:, :, :inner]
    gate_part = projected[:, :, inner:]
    padded = padded_2(inner_part, (("row", 0), ("col", 1)), 1)
    conv_out = conv_silu(padded, conv_weight, conv_bias, rows_here, cols_here)
    count = rows_here * cols_here
    out = mix(
        conv_out.reshape(count, inner),
        gate_part.reshape(count, inner),
        tokens.reshape(count, width),
        tissue.astype(jnp.float32).reshape(count, 1),
        proj_weight,
        dt_weight,
        dt_bias,
        a_rate.transpose(0, 2, 1) * (-1.0 / math.log(2.0)),
        skip_d,
        out_gain.reshape(1, inner),
        out_weight,
        rows_here,
        cols_here,
    )
    return out.reshape(rows_here, cols_here, width)


def solution(mesh):
    return jax.shard_map(
        local,
        mesh=mesh,
        in_specs=(
            P("row", "col", None),
            P("row", "col"),
            P(),
            P(),
            P(),
            P(),
            P(),
            P(),
            P(),
            P(),
            P(),
            P(),
            P(),
        ),
        out_specs=P("row", "col", None),
        check_vma=False,
    )
```

```python
import functools
import math

import jax
import jax.numpy as jnp
from jax import lax
from jax.experimental import pallas as pl
from jax.experimental.pallas import tpu as pltpu
from jax.sharding import PartitionSpec as P

LANES = 128
GROUP = 8
STAGGER = 3
SPAN = 4
MESH = pl.DeviceIdType.MESH


def spread_out(rows, cols, rank, nstate, pj, pk, ex):
    count = rows * cols

    def reorder(i, _):
        t, g = i // (rows // GROUP), i % (rows // GROUP)
        source = pl.ds(g * (GROUP * cols) + t, GROUP, stride=cols)
        target = pl.ds(pl.multiple_of(t * rows + g * GROUP, GROUP), GROUP)
        for k in (0, 2):
            ex[k, 0, target, :] = pj[k, source, :]
        return 0

    lax.fori_loop(0, count // GROUP, reorder, 0)
    for k in range(4):
        for c in range(count // 128):
            at = pl.ds(c * 128, 128)
            value = pj[k, at, :] if k % 2 else ex[k, 0, at, :]
            high = value.astype(jnp.bfloat16)
            low = (value - high.astype(jnp.float32)).astype(jnp.bfloat16)
            pk[k, at, :LANES] = high
            pk[k, at, LANES:] = low

    source = lax.broadcasted_iota(jnp.int32, (2 * LANES, 2 * LANES), 0) % LANES
    target = lax.broadcasted_iota(jnp.int32, (2 * LANES, 2 * LANES), 1) // LANES

    def pair(m, _):
        pick = (source == target + (rank + 2 * m)).astype(jnp.bfloat16)
        for k in range(4):
            for c in range(count // 256):
                at = pl.ds(c * 256, 256)
                value = jnp.dot(pk[k, at, :], pick, preferred_element_type=jnp.float32)
                ex[k, 2 * m, at, :] = value[:, :LANES]
                ex[k, 2 * m + 1, at, :] = value[:, LANES:]
        return 0

    lax.fori_loop(0, nstate, pair, 0)


def scan_kernel(
    rows, cols, tok_ref, lng_ref, inw_ref, cw_ref, cb_ref, tis_ref, proj_ref, dtw_ref, dtb_ref, rate_ref, skip_ref,
    og_ref, ow_ref, out_ref,
    edge, halo, hin, pad, gate_ref, x_ref, hs, hr, xs, dl, pj, ys, st, sbuf, rbuf, ssem, rsem, *wide_refs
):
    nrow, ncol = lax.axis_size("row"), lax.axis_size("col")
    me_row, me_col = lax.axis_index("row"), lax.axis_index("col")
    count, inner = x_ref.shape
    tiles = inner // LANES
    rank = dtw_ref.shape[1]
    nstate = rate_ref.shape[1]

    barrier = pltpu.get_barrier_semaphore()
    last = count - cols
    sends = (
        (1, 0, tok_ref.at[pl.ds(last, cols)], 0, cols),
        (-1, 0, tok_ref.at[pl.ds(0, cols)], cols, cols),
        (0, 1, edge.at[1], 2 * cols, rows),
        (0, -1, edge.at[0], 2 * cols + rows, rows),
        (1, 1, tok_ref.at[pl.ds(count - 16, 16)], 2 * cols + 2 * rows, 16),
        (1, -1, tok_ref.at[pl.ds(last, 16)], 2 * cols + 2 * rows + 16, 16),
        (-1, 1, tok_ref.at[pl.ds(cols - 16, 16)], 2 * cols + 2 * rows + 32, 16),
        (-1, -1, tok_ref.at[pl.ds(0, 16)], 2 * cols + 2 * rows + 48, 16),
    )

    def there(dr, dc):
        r, c = me_row + dr, me_col + dc
        return (r >= 0) & (r < nrow) & (c >= 0) & (c < ncol)

    expected = 0
    for dr, dc, _, _, _ in sends:
        expected = expected + there(dr, dc).astype(jnp.int32)

        @pl.when(there(dr, dc))
        def _():
            pl.semaphore_signal(
                barrier, inc=1, device_id=(me_row + dr, me_col + dc), device_id_type=MESH
            )

    for side in range(2):
        want = lax.broadcasted_iota(jnp.int32, (rows, count), 0) * cols + side * (cols - 1)
        pick = (lax.broadcasted_iota(jnp.int32, (rows, count), 1) == want).astype(jnp.bfloat16)
        edge[side] = jnp.dot(pick, tok_ref[...], preferred_element_type=jnp.float32).astype(
            jnp.bfloat16
        )

    pl.semaphore_wait(barrier, expected)

    def border(which):
        dr, dc, source, start, size = sends[which]
        return pltpu.make_async_remote_copy(
            src_ref=source,
            dst_ref=halo.at[pl.ds(start, size)],
            send_sem=hs.at[which],
            recv_sem=hr.at[which],
            device_id=(me_row + dr, me_col + dc),
            device_id_type=MESH,
        )

    for which, (dr, dc, _, _, _) in enumerate(sends):

        @pl.when(there(dr, dc))
        def _():
            border(which).start()

    step = min(count, 128)

    def normed(block):
        return layer_norm(block.astype(jnp.float32), lng_ref[...]).astype(jnp.bfloat16)

    def project(c, _):
        at = pl.ds(pl.multiple_of(c * step, step), step)
        both = jnp.dot(normed(tok_ref[at, :]), inw_ref[...], preferred_element_type=jnp.float32)
        both = both.astype(jnp.bfloat16)
        gate_ref[at, :] = both[:, inner:]
        part = both[:, :inner].astype(jnp.float32).reshape(step // cols, cols, inner)
        pad[pl.ds(1 + c * (step // cols), step // cols), GROUP : GROUP + cols, :] = part
        return 0

    lax.fori_loop(0, count // step, project, 0)

    for which, (dr, dc, _, start, size) in enumerate(sends):

        @pl.when(there(-dr, -dc))
        def _():
            border(which).wait_recv()

        @pl.when(jnp.logical_not(there(-dr, -dc)))
        def _():
            halo[pl.ds(start, size), :] = jnp.zeros((size, halo.shape[1]), jnp.bfloat16)

    around = jnp.dot(normed(halo[...]), inw_ref[:, :inner], preferred_element_type=jnp.float32)
    hin[...] = around.astype(jnp.bfloat16).astype(jnp.float32)
    pad[0, GROUP : GROUP + cols, :] = hin[0:cols, :]
    pad[rows + 1, GROUP : GROUP + cols, :] = hin[cols : 2 * cols, :]
    low, high = pl.ds(GROUP - 1, 1), pl.ds(GROUP + cols, 1)

    def sides(r, _):
        pad[r + 1, low, :] = hin[pl.ds(2 * cols + r, 1), :]
        pad[r + 1, high, :] = hin[pl.ds(2 * cols + rows + r, 1), :]
        return 0

    lax.fori_loop(0, rows, sides, 0)
    corner = 2 * cols + 2 * rows
    pad[0, low, :] = hin[pl.ds(corner + 15, 1), :]
    pad[0, high, :] = hin[pl.ds(corner + 16, 1), :]
    pad[rows + 1, low, :] = hin[pl.ds(corner + 47, 1), :]
    pad[rows + 1, high, :] = hin[pl.ds(corner + 48, 1), :]
    taps = cw_ref[...].astype(jnp.float32)

    def filtered(r, _):
        total = jnp.broadcast_to(cb_ref[...], (cols, inner))
        for i in range(3):
            for j in range(3):
                window = pad[r + i, GROUP - 1 + j : GROUP - 1 + j + cols, :]
                total = total + window * taps[3 * i + j : 3 * i + j + 1, :]
        total = total * jax.nn.sigmoid(total)
        x_ref[pl.ds(pl.multiple_of(r * cols, cols), cols), :] = total.astype(jnp.bfloat16)
        return 0

    lax.fori_loop(0, rows, filtered, 0)

    def prepare(c, _):
        at = pl.ds(pl.multiple_of(c * step, step), step)
        block = x_ref[at, :]
        wide = block.astype(jnp.float32)
        mask = tis_ref[at, :]
        skip = jnp.sum(skip_ref[...], axis=0, keepdims=True)
        base = wide * skip
        for e in range(tiles):
            xs[e, at, :] = wide[:, e * LANES : (e + 1) * LANES]
            ys[e, at, :] = base[:, e * LANES : (e + 1) * LANES]
        for k in range(4):
            p = jnp.dot(block, proj_ref[k], preferred_element_type=jnp.float32)
            pj[k, at, :] = jnp.concatenate(
                [p, jnp.zeros((step, LANES - p.shape[1]), jnp.float32)], axis=1
            )
            low = p[:, :rank].astype(jnp.bfloat16)
            z = jnp.dot(low, dtw_ref[k], preferred_element_type=jnp.float32) + dtb_ref[k : k + 1, :]
            delta = (jnp.maximum(z, 0.0) + jnp.log1p(jnp.exp(-jnp.abs(z)))) * mask
            for e in range(tiles):
                dl[k * tiles + e, at, :] = delta[:, e * LANES : (e + 1) * LANES]
        return 0

    lax.fori_loop(0, count // step, prepare, 0)

    if wide_refs:
        spread_out(rows, cols, rank, nstate, pj, *wide_refs)
    row_units, col_units = rows // GROUP * tiles, cols // GROUP * tiles
    plans = (
        (0, me_col, (me_row, me_col + 1), ncol, row_units, 0),
        (2, ncol - 1 - me_col, (me_row, me_col - 1), ncol, row_units, row_units),
        (1, me_row, (me_row + 1, me_col), nrow, col_units, 2 * row_units),
        (3, nrow - 1 - me_row, (me_row - 1, me_col), nrow, col_units, 2 * row_units + col_units),
    )

    def copy_of(u, device):
        return pltpu.make_async_remote_copy(
            src_ref=sbuf.at[u],
            dst_ref=rbuf.at[u],
            send_sem=ssem.at[u],
            recv_sem=rsem.at[u],
            device_id=device,
            device_id_type=MESH,
        )

    def unit(k, ahead, device, size, first, q):
        g = q // tiles
        e = q % tiles
        u = first + q
        length = cols if k % 2 == 0 else rows

        @pl.when(ahead > 0)
        def _():
            copy_of(u, device).wait_recv()
            st[...] = rbuf[u].astype(jnp.float32)

        @pl.when(ahead == 0)
        def _():
            st[...] = jnp.zeros_like(st)

        rates = [
            jnp.broadcast_to(
                rate_ref[k, n : n + 1, pl.ds(pl.multiple_of(e * LANES, LANES), LANES)],
                (GROUP, LANES),
            )
            for n in range(nstate)
        ]
        lane = k * tiles + e

        def advance(block, state):
            state = list(state)
            for sub in range(SPAN):
                t = block * SPAN + sub
                if k >= 2:
                    t = length - 1 - t
                if k % 2 == 0:
                    at = pl.ds(g * (GROUP * cols) + t, GROUP, stride=cols)
                else:
                    at = pl.ds(pl.multiple_of(t * cols + g * GROUP, GROUP), GROUP)
                d = dl[lane, at, :]
                dx = d * xs[e, at, :]
                if wide_refs:
                    ex = wide_refs[1]
                    where = at
                    if k % 2 == 0:
                        where = pl.ds(pl.multiple_of(t * rows + g * GROUP, GROUP), GROUP)
                    wide = [ex[k, m, where, :] for m in range(2 * nstate)]
                else:
                    p = pj[k, at, :]
                    wide = [
                        jnp.broadcast_to(p[:, rank + m : rank + m + 1], (GROUP, LANES))
                        for m in range(2 * nstate)
                    ]
                parts = [None] * 4
                for n in range(nstate):
                    state[n] = jnp.exp2(d * rates[n]) * state[n] + dx * wide[n]
                    term = state[n] * wide[nstate + n]
                    parts[n % 4] = term if parts[n % 4] is None else parts[n % 4] + term
                ys[e, at, :] += (parts[0] + parts[1]) + (parts[2] + parts[3])
            return tuple(state)

        state = tuple(st[n * GROUP : (n + 1) * GROUP, :] for n in range(nstate))
        state = lax.fori_loop(0, length // SPAN, advance, state)

        @pl.when(ahead < size - 1)
        def _():
            sbuf[u] = jnp.concatenate(state, axis=0).astype(jnp.bfloat16)
            copy_of(u, device).start()

    slots = max(STAGGER * (ncol - 1) + row_units, STAGGER * (nrow - 1) + col_units)

    def slot(s, _):
        for k, ahead, device, size, units, first in plans:
            q = s - STAGGER * ahead

            @pl.when((q >= 0) & (q < units))
            def _():
                unit(k, ahead, device, size, first, q)

        return 0

    lax.fori_loop(0, slots, slot, 0)

    def finish(c, _):
        at = pl.ds(pl.multiple_of(c * step, step), step)
        parts = [ys[e, at, :] for e in range(tiles)]
        mean = sum(jnp.sum(a, axis=1, keepdims=True) for a in parts) / inner
        parts = [a - mean for a in parts]
        spread = sum(jnp.sum(a * a, axis=1, keepdims=True) for a in parts) / inner
        scale = lax.rsqrt(spread + 1e-05)
        gate = gate_ref[at, :].astype(jnp.float32)
        gate = gate * jax.nn.sigmoid(gate) * og_ref[...]
        mixed = (jnp.concatenate(parts, axis=1) * scale * gate).astype(jnp.bfloat16)
        branch = jnp.dot(mixed, ow_ref[...], preferred_element_type=jnp.float32)
        out_ref[at, :] = (tok_ref[at, :].astype(jnp.float32) + tis_ref[at, :] * branch).astype(
            jnp.bfloat16
        )
        return 0

    lax.fori_loop(0, count // step, finish, 0)

    for which, (dr, dc, _, _, _) in enumerate(sends):

        @pl.when(there(dr, dc))
        def _():
            border(which).wait_send()

    for k, ahead, device, size, units, first in plans:

        @pl.when(ahead < size - 1)
        def _():
            def drain(q, _):
                copy_of(first + q, device).wait_send()
                return 0

            lax.fori_loop(0, units, drain, 0)


def mix(tokens, gain, inw, taps, bias, tissue, proj, dtw, dtb, rate, skip, og, ow, rows, cols):
    count, width = tokens.shape
    inner = inw.shape[1] // 2
    tiles = inner // LANES
    nstate = rate.shape[1]
    units = 2 * tiles * (rows // GROUP + cols // GROUP)
    wide_shapes = []
    if count <= 512 and count % 256 == 0:
        wide_shapes = [
            pltpu.VMEM((4, count, 2 * LANES), jnp.bfloat16),
            pltpu.VMEM((4, 2 * nstate, count, LANES), jnp.float32),
        ]
    held = (units, nstate * GROUP, LANES)
    return pl.pallas_call(
        functools.partial(scan_kernel, rows, cols),
        out_shape=jax.ShapeDtypeStruct((count, ow.shape[1]), jnp.bfloat16),
        in_specs=[pl.BlockSpec(memory_space=pltpu.VMEM)] * 13,
        out_specs=pl.BlockSpec(memory_space=pltpu.VMEM),
        scratch_shapes=[
            pltpu.VMEM((2, rows, width), jnp.bfloat16),
            pltpu.VMEM((2 * rows + 2 * cols + 64, width), jnp.bfloat16),
            pltpu.VMEM((2 * rows + 2 * cols + 64, inner), jnp.float32),
            pltpu.VMEM((rows + 2, cols + 2 * GROUP, inner), jnp.float32),
            pltpu.VMEM((count, inner), jnp.bfloat16),
            pltpu.VMEM((count, inner), jnp.bfloat16),
            pltpu.SemaphoreType.DMA((8,)),
            pltpu.SemaphoreType.DMA((8,)),
            pltpu.VMEM((tiles, count, LANES), jnp.float32),
            pltpu.VMEM((4 * tiles, count, LANES), jnp.float32),
            pltpu.VMEM((4, count, LANES), jnp.float32),
            pltpu.VMEM((tiles, count, LANES), jnp.float32),
            pltpu.VMEM((nstate * GROUP, LANES), jnp.float32),
            pltpu.VMEM(held, jnp.bfloat16),
            pltpu.VMEM(held, jnp.bfloat16),
            pltpu.SemaphoreType.DMA((units,)),
            pltpu.SemaphoreType.DMA((units,)),
            *wide_shapes,
        ],
        compiler_params=pltpu.CompilerParams(
            collective_id=0, has_side_effects=True, vmem_limit_bytes=56 * 1024 * 1024
        ),
    )(tokens, gain, inw, taps, bias, tissue, proj, dtw, dtb, rate, skip, og, ow)


def layer_norm(values, gain):
    center = values - jnp.mean(values, axis=-1, keepdims=True)
    spread = jnp.mean(center * center, axis=-1, keepdims=True)
    return center * lax.rsqrt(spread + 1e-05) * gain


def local(
    tokens,
    tissue,
    ln_gain,
    in_weight,
    conv_weight,
    conv_bias,
    proj_weight,
    dt_weight,
    dt_bias,
    a_rate,
    skip_d,
    out_gain,
    out_weight,
):
    rows_here, cols_here, width = tokens.shape
    inner = in_weight.shape[1] // 2
    count = rows_here * cols_here
    out = mix(
        tokens.reshape(count, width),
        ln_gain.reshape(1, width),
        in_weight,
        conv_weight.reshape(9, inner),
        conv_bias.reshape(1, inner),
        tissue.astype(jnp.float32).reshape(count, 1),
        proj_weight,
        dt_weight,
        dt_bias,
        a_rate.transpose(0, 2, 1) * (-1.0 / math.log(2.0)),
        skip_d,
        out_gain.reshape(1, inner),
        out_weight,
        rows_here,
        cols_here,
    )
    return out.reshape(rows_here, cols_here, width)


def solution(mesh):
    return jax.shard_map(
        local,
        mesh=mesh,
        in_specs=(
            P("row", "col", None),
            P("row", "col"),
            P(),
            P(),
            P(),
            P(),
            P(),
            P(),
            P(),
            P(),
            P(),
            P(),
            P(),
        ),
        out_specs=P("row", "col", None),
        check_vma=False,
    )
```

```python
import functools
import math

import jax
import jax.numpy as jnp
from jax import lax
from jax.experimental import pallas as pl
from jax.experimental.pallas import tpu as pltpu
from jax.sharding import PartitionSpec as P

LANES = 128
GROUP = 8
STAGGER = 3
SPAN = 4
MESH = pl.DeviceIdType.MESH


def spread_pair(m, directions, rank, count, pk, ex):
    source = lax.broadcasted_iota(jnp.int32, (2 * LANES, 2 * LANES), 0) % LANES
    target = lax.broadcasted_iota(jnp.int32, (2 * LANES, 2 * LANES), 1) // LANES
    pick = (source == target + (rank + 2 * m)).astype(jnp.bfloat16)
    for k in directions:
        for c in range(count // 256):
            at = pl.ds(c * 256, 256)
            value = jnp.dot(pk[k, at, :], pick, preferred_element_type=jnp.float32)
            ex[k, 2 * m, at, :] = value[:, :LANES]
            ex[k, 2 * m + 1, at, :] = value[:, LANES:]


def spread_out(rows, cols, rank, nstate, pj, pk, ex):
    count = rows * cols

    def reorder(i, _):
        t, g = i // (rows // GROUP), i % (rows // GROUP)
        source = pl.ds(g * (GROUP * cols) + t, GROUP, stride=cols)
        target = pl.ds(pl.multiple_of(t * rows + g * GROUP, GROUP), GROUP)
        for k in (0, 2):
            ex[k, 0, target, :] = pj[k, source, :]
        return 0

    lax.fori_loop(0, count // GROUP, reorder, 0)
    for k in range(4):
        for c in range(count // 128):
            at = pl.ds(c * 128, 128)
            value = pj[k, at, :] if k % 2 else ex[k, 0, at, :]
            high = value.astype(jnp.bfloat16)
            low = (value - high.astype(jnp.float32)).astype(jnp.bfloat16)
            pk[k, at, :LANES] = high
            pk[k, at, LANES:] = low

    def pair(m, _):
        spread_pair(m, (0, 2), rank, count, pk, ex)
        return 0

    lax.fori_loop(0, nstate, pair, 0)


def scan_kernel(
    rows, cols, tok_ref, lng_ref, inw_ref, cw_ref, cb_ref, tis_ref, proj_ref, dtw_ref, dtb_ref, rate_ref, skip_ref,
    og_ref, ow_ref, out_ref,
    edge, halo, hin, pad, gate_ref, x_ref, hs, hr, xs, dl, pj, ys, st, sbuf, rbuf, ssem, rsem, *wide_refs
):
    nrow, ncol = lax.axis_size("row"), lax.axis_size("col")
    me_row, me_col = lax.axis_index("row"), lax.axis_index("col")
    count, inner = x_ref.shape
    tiles = inner // LANES
    rank = dtw_ref.shape[1]
    nstate = rate_ref.shape[1]

    barrier = pltpu.get_barrier_semaphore()
    last = count - cols
    sends = (
        (1, 0, tok_ref.at[pl.ds(last, cols)], 0, cols),
        (-1, 0, tok_ref.at[pl.ds(0, cols)], cols, cols),
        (0, 1, edge.at[1], 2 * cols, rows),
        (0, -1, edge.at[0], 2 * cols + rows, rows),
        (1, 1, tok_ref.at[pl.ds(count - 16, 16)], 2 * cols + 2 * rows, 16),
        (1, -1, tok_ref.at[pl.ds(last, 16)], 2 * cols + 2 * rows + 16, 16),
        (-1, 1, tok_ref.at[pl.ds(cols - 16, 16)], 2 * cols + 2 * rows + 32, 16),
        (-1, -1, tok_ref.at[pl.ds(0, 16)], 2 * cols + 2 * rows + 48, 16),
    )

    def there(dr, dc):
        r, c = me_row + dr, me_col + dc
        return (r >= 0) & (r < nrow) & (c >= 0) & (c < ncol)

    expected = 0
    for dr, dc, _, _, _ in sends:
        expected = expected + there(dr, dc).astype(jnp.int32)

        @pl.when(there(dr, dc))
        def _():
            pl.semaphore_signal(
                barrier, inc=1, device_id=(me_row + dr, me_col + dc), device_id_type=MESH
            )

    for side in range(2):
        want = lax.broadcasted_iota(jnp.int32, (rows, count), 0) * cols + side * (cols - 1)
        pick = (lax.broadcasted_iota(jnp.int32, (rows, count), 1) == want).astype(jnp.bfloat16)
        edge[side] = jnp.dot(pick, tok_ref[...], preferred_element_type=jnp.float32).astype(
            jnp.bfloat16
        )

    pl.semaphore_wait(barrier, expected)

    def border(which):
        dr, dc, source, start, size = sends[which]
        return pltpu.make_async_remote_copy(
            src_ref=source,
            dst_ref=halo.at[pl.ds(start, size)],
            send_sem=hs.at[which],
            recv_sem=hr.at[which],
            device_id=(me_row + dr, me_col + dc),
            device_id_type=MESH,
        )

    for which, (dr, dc, _, _, _) in enumerate(sends):

        @pl.when(there(dr, dc))
        def _():
            border(which).start()

    step = min(count, 128)

    def normed(block):
        return layer_norm(block.astype(jnp.float32), lng_ref[...]).astype(jnp.bfloat16)

    def project(c, _):
        at = pl.ds(pl.multiple_of(c * step, step), step)
        both = jnp.dot(normed(tok_ref[at, :]), inw_ref[...], preferred_element_type=jnp.float32)
        both = both.astype(jnp.bfloat16)
        gate_ref[at, :] = both[:, inner:]
        part = both[:, :inner].astype(jnp.float32).reshape(step // cols, cols, inner)
        pad[pl.ds(1 + c * (step // cols), step // cols), GROUP : GROUP + cols, :] = part
        return 0

    lax.fori_loop(0, count // step, project, 0)

    for which, (dr, dc, _, start, size) in enumerate(sends):

        @pl.when(there(-dr, -dc))
        def _():
            border(which).wait_recv()

        @pl.when(jnp.logical_not(there(-dr, -dc)))
        def _():
            halo[pl.ds(start, size), :] = jnp.zeros((size, halo.shape[1]), jnp.bfloat16)

    around = jnp.dot(normed(halo[...]), inw_ref[:, :inner], preferred_element_type=jnp.float32)
    hin[...] = around.astype(jnp.bfloat16).astype(jnp.float32)
    pad[0, GROUP : GROUP + cols, :] = hin[0:cols, :]
    pad[rows + 1, GROUP : GROUP + cols, :] = hin[cols : 2 * cols, :]
    low, high = pl.ds(GROUP - 1, 1), pl.ds(GROUP + cols, 1)

    def sides(r, _):
        pad[r + 1, low, :] = hin[pl.ds(2 * cols + r, 1), :]
        pad[r + 1, high, :] = hin[pl.ds(2 * cols + rows + r, 1), :]
        return 0

    lax.fori_loop(0, rows, sides, 0)
    corner = 2 * cols + 2 * rows
    pad[0, low, :] = hin[pl.ds(corner + 15, 1), :]
    pad[0, high, :] = hin[pl.ds(corner + 16, 1), :]
    pad[rows + 1, low, :] = hin[pl.ds(corner + 47, 1), :]
    pad[rows + 1, high, :] = hin[pl.ds(corner + 48, 1), :]
    taps = cw_ref[...].astype(jnp.float32)

    def filtered(r, _):
        total = jnp.broadcast_to(cb_ref[...], (cols, inner))
        for i in range(3):
            for j in range(3):
                window = pad[r + i, GROUP - 1 + j : GROUP - 1 + j + cols, :]
                total = total + window * taps[3 * i + j : 3 * i + j + 1, :]
        total = total * jax.nn.sigmoid(total)
        x_ref[pl.ds(pl.multiple_of(r * cols, cols), cols), :] = total.astype(jnp.bfloat16)
        return 0

    lax.fori_loop(0, rows, filtered, 0)

    def prepare(c, _):
        at = pl.ds(pl.multiple_of(c * step, step), step)
        block = x_ref[at, :]
        wide = block.astype(jnp.float32)
        mask = tis_ref[at, :]
        skip = jnp.sum(skip_ref[...], axis=0, keepdims=True)
        base = wide * skip
        for e in range(tiles):
            xs[e, at, :] = wide[:, e * LANES : (e + 1) * LANES]
            ys[e, at, :] = base[:, e * LANES : (e + 1) * LANES]
        for k in range(4):
            p = jnp.dot(block, proj_ref[k], preferred_element_type=jnp.float32)
            pj[k, at, :] = jnp.concatenate(
                [p, jnp.zeros((step, LANES - p.shape[1]), jnp.float32)], axis=1
            )
            low = p[:, :rank].astype(jnp.bfloat16)
            z = jnp.dot(low, dtw_ref[k], preferred_element_type=jnp.float32) + dtb_ref[k : k + 1, :]
            delta = (jnp.maximum(z, 0.0) + jnp.log1p(jnp.exp(-jnp.abs(z)))) * mask
            for e in range(tiles):
                dl[k * tiles + e, at, :] = delta[:, e * LANES : (e + 1) * LANES]
        return 0

    lax.fori_loop(0, count // step, prepare, 0)

    if wide_refs:
        spread_out(rows, cols, rank, nstate, pj, *wide_refs)
    row_units, col_units = rows // GROUP * tiles, cols // GROUP * tiles
    plans = (
        (0, me_col, (me_row, me_col + 1), ncol, row_units, 0),
        (2, ncol - 1 - me_col, (me_row, me_col - 1), ncol, row_units, row_units),
        (1, me_row, (me_row + 1, me_col), nrow, col_units, 2 * row_units),
        (3, nrow - 1 - me_row, (me_row - 1, me_col), nrow, col_units, 2 * row_units + col_units),
    )

    def copy_of(u, device):
        return pltpu.make_async_remote_copy(
            src_ref=sbuf.at[u],
            dst_ref=rbuf.at[u],
            send_sem=ssem.at[u],
            recv_sem=rsem.at[u],
            device_id=device,
            device_id_type=MESH,
        )

    def unit(k, ahead, device, size, first, q):
        g = q // tiles
        e = q % tiles
        u = first + q
        length = cols if k % 2 == 0 else rows

        @pl.when(ahead > 0)
        def _():
            copy_of(u, device).wait_recv()
            st[...] = rbuf[u].astype(jnp.float32)

        @pl.when(ahead == 0)
        def _():
            st[...] = jnp.zeros_like(st)

        rates = [
            jnp.broadcast_to(
                rate_ref[k, n : n + 1, pl.ds(pl.multiple_of(e * LANES, LANES), LANES)],
                (GROUP, LANES),
            )
            for n in range(nstate)
        ]
        lane = k * tiles + e

        def advance(block, state):
            state = list(state)
            for sub in range(SPAN):
                t = block * SPAN + sub
                if k >= 2:
                    t = length - 1 - t
                if k % 2 == 0:
                    at = pl.ds(g * (GROUP * cols) + t, GROUP, stride=cols)
                else:
                    at = pl.ds(pl.multiple_of(t * cols + g * GROUP, GROUP), GROUP)
                d = dl[lane, at, :]
                dx = d * xs[e, at, :]
                if wide_refs:
                    ex = wide_refs[1]
                    where = at
                    if k % 2 == 0:
                        where = pl.ds(pl.multiple_of(t * rows + g * GROUP, GROUP), GROUP)
                    wide = [ex[k, m, where, :] for m in range(2 * nstate)]
                else:
                    p = pj[k, at, :]
                    wide = [
                        jnp.broadcast_to(p[:, rank + m : rank + m + 1], (GROUP, LANES))
                        for m in range(2 * nstate)
                    ]
                parts = [None] * 4
                for n in range(nstate):
                    state[n] = jnp.exp2(d * rates[n]) * state[n] + dx * wide[n]
                    term = state[n] * wide[nstate + n]
                    parts[n % 4] = term if parts[n % 4] is None else parts[n % 4] + term
                ys[e, at, :] += (parts[0] + parts[1]) + (parts[2] + parts[3])
            return tuple(state)

        state = tuple(st[n * GROUP : (n + 1) * GROUP, :] for n in range(nstate))
        state = lax.fori_loop(0, length // SPAN, advance, state)

        @pl.when(ahead < size - 1)
        def _():
            sbuf[u] = jnp.concatenate(state, axis=0).astype(jnp.bfloat16)
            copy_of(u, device).start()

    later = nstate if wide_refs else 0
    slots = max(STAGGER * (ncol - 1) + row_units, STAGGER * (nrow - 1) + col_units + later)

    def slot(s, _):
        for k, ahead, device, size, units, first in plans:
            q = s - STAGGER * ahead - (later if k % 2 else 0)

            @pl.when((q >= 0) & (q < units))
            def _():
                unit(k, ahead, device, size, first, q)

        if wide_refs:

            @pl.when(s < nstate)
            def _():
                spread_pair(s, (1, 3), rank, count, *wide_refs)

        return 0

    lax.fori_loop(0, slots, slot, 0)

    def finish(c, _):
        at = pl.ds(pl.multiple_of(c * step, step), step)
        parts = [ys[e, at, :] for e in range(tiles)]
        mean = sum(jnp.sum(a, axis=1, keepdims=True) for a in parts) / inner
        parts = [a - mean for a in parts]
        spread = sum(jnp.sum(a * a, axis=1, keepdims=True) for a in parts) / inner
        scale = lax.rsqrt(spread + 1e-05)
        gate = gate_ref[at, :].astype(jnp.float32)
        gate = gate * jax.nn.sigmoid(gate) * og_ref[...]
        mixed = (jnp.concatenate(parts, axis=1) * scale * gate).astype(jnp.bfloat16)
        branch = jnp.dot(mixed, ow_ref[...], preferred_element_type=jnp.float32)
        out_ref[at, :] = (tok_ref[at, :].astype(jnp.float32) + tis_ref[at, :] * branch).astype(
            jnp.bfloat16
        )
        return 0

    lax.fori_loop(0, count // step, finish, 0)

    for which, (dr, dc, _, _, _) in enumerate(sends):

        @pl.when(there(dr, dc))
        def _():
            border(which).wait_send()

    for k, ahead, device, size, units, first in plans:

        @pl.when(ahead < size - 1)
        def _():
            def drain(q, _):
                copy_of(first + q, device).wait_send()
                return 0

            lax.fori_loop(0, units, drain, 0)


def mix(tokens, gain, inw, taps, bias, tissue, proj, dtw, dtb, rate, skip, og, ow, rows, cols):
    count, width = tokens.shape
    inner = inw.shape[1] // 2
    tiles = inner // LANES
    nstate = rate.shape[1]
    units = 2 * tiles * (rows // GROUP + cols // GROUP)
    wide_shapes = []
    if count <= 512 and count % 256 == 0:
        wide_shapes = [
            pltpu.VMEM((4, count, 2 * LANES), jnp.bfloat16),
            pltpu.VMEM((4, 2 * nstate, count, LANES), jnp.float32),
        ]
    held = (units, nstate * GROUP, LANES)
    return pl.pallas_call(
        functools.partial(scan_kernel, rows, cols),
        out_shape=jax.ShapeDtypeStruct((count, ow.shape[1]), jnp.bfloat16),
        in_specs=[pl.BlockSpec(memory_space=pltpu.VMEM)] * 13,
        out_specs=pl.BlockSpec(memory_space=pltpu.VMEM),
        scratch_shapes=[
            pltpu.VMEM((2, rows, width), jnp.bfloat16),
            pltpu.VMEM((2 * rows + 2 * cols + 64, width), jnp.bfloat16),
            pltpu.VMEM((2 * rows + 2 * cols + 64, inner), jnp.float32),
            pltpu.VMEM((rows + 2, cols + 2 * GROUP, inner), jnp.float32),
            pltpu.VMEM((count, inner), jnp.bfloat16),
            pltpu.VMEM((count, inner), jnp.bfloat16),
            pltpu.SemaphoreType.DMA((8,)),
            pltpu.SemaphoreType.DMA((8,)),
            pltpu.VMEM((tiles, count, LANES), jnp.float32),
            pltpu.VMEM((4 * tiles, count, LANES), jnp.float32),
            pltpu.VMEM((4, count, LANES), jnp.float32),
            pltpu.VMEM((tiles, count, LANES), jnp.float32),
            pltpu.VMEM((nstate * GROUP, LANES), jnp.float32),
            pltpu.VMEM(held, jnp.bfloat16),
            pltpu.VMEM(held, jnp.bfloat16),
            pltpu.SemaphoreType.DMA((units,)),
            pltpu.SemaphoreType.DMA((units,)),
            *wide_shapes,
        ],
        compiler_params=pltpu.CompilerParams(
            collective_id=0, has_side_effects=True, vmem_limit_bytes=56 * 1024 * 1024
        ),
    )(tokens, gain, inw, taps, bias, tissue, proj, dtw, dtb, rate, skip, og, ow)


def layer_norm(values, gain):
    center = values - jnp.mean(values, axis=-1, keepdims=True)
    spread = jnp.mean(center * center, axis=-1, keepdims=True)
    return center * lax.rsqrt(spread + 1e-05) * gain


def local(
    tokens,
    tissue,
    ln_gain,
    in_weight,
    conv_weight,
    conv_bias,
    proj_weight,
    dt_weight,
    dt_bias,
    a_rate,
    skip_d,
    out_gain,
    out_weight,
):
    rows_here, cols_here, width = tokens.shape
    inner = in_weight.shape[1] // 2
    count = rows_here * cols_here
    out = mix(
        tokens.reshape(count, width),
        ln_gain.reshape(1, width),
        in_weight,
        conv_weight.reshape(9, inner),
        conv_bias.reshape(1, inner),
        tissue.astype(jnp.float32).reshape(count, 1),
        proj_weight,
        dt_weight,
        dt_bias,
        a_rate.transpose(0, 2, 1) * (-1.0 / math.log(2.0)),
        skip_d,
        out_gain.reshape(1, inner),
        out_weight,
        rows_here,
        cols_here,
    )
    return out.reshape(rows_here, cols_here, width)


def solution(mesh):
    return jax.shard_map(
        local,
        mesh=mesh,
        in_specs=(
            P("row", "col", None),
            P("row", "col"),
            P(),
            P(),
            P(),
            P(),
            P(),
            P(),
            P(),
            P(),
            P(),
            P(),
            P(),
        ),
        out_specs=P("row", "col", None),
        check_vma=False,
    )
```
